32 devices in a mesh: groups: 2 (over y), patch: 16 (over z, x, core).
Axes of the slice: x: 2, y: 2, z: 4, core: 2. Of those that a mesh axis runs over, the one named last changes fastest.
Arguments:
- img_q: bfloat16 [256, 1536], P(('groups', 'patch')), parts along dimension 0, may hold values from -40 to 40
- img_kv: bfloat16 [2, 256, 1536], P(None, ('groups', 'patch')), parts along dimension 1, may hold values from -8 to 8
- stale_mant: bfloat16 [2, 256, 1536], P(None, ('groups', 'patch')), parts along dimension 1, may hold values from -2.5 to 2.5
- stale_exp: int32 [2, 256, 12], P(None, ('groups', 'patch')), parts along dimension 1, may hold values from -2 to 1
- txt_q: bfloat16 [512, 1536], P('groups'), parts along dimension 0, may hold values from -48 to 48
- txt_kv: bfloat16 [2, 512, 1536], P(None, 'groups'), parts along dimension 1, may hold values from -8 to 8
- order: int32 [32], P(('groups', 'patch')), parts along dimension 0, may hold values from 0 to 15, as said below
- timestep: int32 [2], P('groups'), parts along dimension 0, may hold values from 0 to 27
- gate_table: float32 [28, 2, 1536], replicated, may hold values from 0.5 to 2
Outputs:
- img_out: bfloat16 [256, 1536], P(('groups', 'patch')), parts along dimension 0
- txt_out: bfloat16 [512, 1536], P('groups'), parts along dimension 0
The draws below stay inside these ranges and needn't reach their ends.
There are 2 independent parts, one for each index of `groups`. The reference program is written for one: setup_inputs(seed, part) draws one part's arguments, and reference() takes and returns one part's arrays. A program takes and returns all parts, laid end to end along the dimension named above; an argument that names none is the same for every part. Nothing has to cross between parts.
Inputs may be any that keep to these rules, and one draw needn't show every extreme that they name: `order`: each patch is held by exactly one device.
All inputs are finite; a program needn't handle non-finite values.
Results may differ from the reference program's by a relative error of at most 0.0063.
Values may be sent and summed in bfloat16 or wider, within the bound.
No kernel may reach another device: no remote copies, remote signals or barrier semaphores. Data moves between devices by JAX's collectives and lax.ppermute only.
A program may use at most 64 MiB of HBM per device.

```python
import jax
import jax.numpy as jnp
from jax import lax

HEADS = 12
HEAD_DIM = 128
TXT = 256
STEPS = 28
TOK_DEV = 8
PATCHES = 16
IMG = 128
WIDTH = 1536


def shared_keys(key, count, salt):
    key = jax.random.fold_in(key, salt)
    return jax.random.normal(key, (count, HEADS * HEAD_DIM), jnp.float32)


def patch_order(key):
    key = jax.random.fold_in(key, 21)
    return jax.random.permutation(key, PATCHES).astype(jnp.int32)


def draw_order(key, part):
    return patch_order(key)


def draw_img_q(key, part):
    key = jax.random.fold_in(key, 1)
    shape = (IMG, HEADS * HEAD_DIM)
    queries = 2.0 * jax.random.normal(key, shape, jnp.float32)
    return queries.astype(jnp.bfloat16)


def draw_img_kv(key, part):
    base = shared_keys(key, IMG, 11)
    key = jax.random.fold_in(key, 2)
    shape = (IMG, HEADS * HEAD_DIM)
    keys = base
    values = jax.random.normal(key, shape, jnp.float32)
    return jnp.stack([keys, values]).astype(jnp.bfloat16)


def draw_txt_q(key, part):
    key = jax.random.fold_in(key, 3)
    shape = (TXT, HEADS * HEAD_DIM)
    queries = 2.0 * jax.random.normal(key, shape, jnp.float32)
    return queries.astype(jnp.bfloat16)


def draw_txt_kv(key, part):
    base = shared_keys(key, TXT, 12)
    key = jax.random.fold_in(key, 4)
    first_key = jax.random.fold_in(key, 0)
    shape = (TXT, HEADS * HEAD_DIM)
    keys = base
    values = jax.random.normal(first_key, shape, jnp.float32)
    return jnp.stack([keys, values]).astype(jnp.bfloat16)


def with_ends(entries, stream_key, least, top_value):
    shape = entries.shape
    place = [jax.random.randint(jax.random.fold_in(stream_key, axis), (), 0, shape[axis]) for axis in range(len(shape))]
    entries = entries.at[tuple(place)].set(least)
    longest = shape.index(max(shape))
    place[longest] = (place[longest] + 1) % shape[longest]
    return entries.at[tuple(place)].set(top_value)


def shard_levels(stream_key, shape, cuts, least, top_value):
    loudness = 1.0
    for dim, parts in cuts:
        heights = jax.random.uniform(jax.random.fold_in(jax.random.fold_in(stream_key, 6), dim), (parts,), jnp.float32, least / len(cuts), top_value / len(cuts))
        loudness = loudness * jnp.repeat(jnp.exp(heights), shape[dim] // parts).reshape((-1,) + (1,) * (len(shape) - 1 - dim))
    return loudness


def bell_draw(key, dims, scale, reach, cuts=(), kind=jnp.bfloat16):
    array = scale * jax.random.normal(key, dims, jnp.float32)
    if cuts:
        array = array * shard_levels(key, dims, cuts, -0.22, 0.18)
    return jnp.clip(array, -reach, reach).astype(kind)


def setup_inputs(seed: int = 0, part: int = 0) -> dict:
    splits = jax.random.split(jax.random.key(seed), 10)
    own_keys = jax.random.split(jax.random.fold_in(splits[9], part), 10)
    return {
        "img_q": draw_img_q(jax.random.fold_in(jax.random.fold_in(splits[9], part), 71), part),
        "img_kv": draw_img_kv(jax.random.fold_in(jax.random.fold_in(splits[9], part), 71), part),
        "stale_mant": bell_draw(own_keys[2], (2, IMG, WIDTH), 0.8, 2.5, ((1, 16),)),
        "stale_exp": with_ends(jax.random.randint(own_keys[3], (2, IMG, HEADS), -2, 2), jax.random.fold_in(own_keys[3], 1), -2, 1).astype(jnp.int32),
        "txt_q": draw_txt_q(jax.random.fold_in(jax.random.fold_in(splits[9], part), 71), part),
        "txt_kv": draw_txt_kv(jax.random.fold_in(jax.random.fold_in(splits[9], part), 71), part),
        "order": draw_order(jax.random.fold_in(jax.random.fold_in(splits[9], part), 71), part),
        "timestep": jax.random.randint(own_keys[7], (1,), 0, STEPS).astype(jnp.int32),
        "gate_table": jnp.clip(jax.random.uniform(splits[8], (STEPS, 2, WIDTH), jnp.float32, 0.5, 2.0), 0.5, 2.0),
    }


def rotate_rows(values, position):
    count = values.shape[0]
    half = HEAD_DIM // 2
    frequency = 10000.0 ** (-jnp.arange(half, dtype=jnp.float32) / half)
    angles = position[:, None] * frequency[None, :]
    cosine = jnp.cos(angles)[:, None, :]
    sine = jnp.sin(angles)[:, None, :]
    split_heads = values.astype(jnp.float32).reshape(count, HEADS, HEAD_DIM)
    first_half = split_heads[..., :half]
    second_half = split_heads[..., half:]
    turned = jnp.concatenate([first_half * cosine - second_half * sine, first_half * sine + second_half * cosine], axis=-1)
    return turned.reshape(count, HEADS * HEAD_DIM).astype(jnp.bfloat16)


def attend(queries, keys, values):
    query_count = queries.shape[0]
    key_count = keys.shape[0]
    q_heads = queries.astype(jnp.float32).reshape(query_count, HEADS, HEAD_DIM)
    k_heads = keys.astype(jnp.float32).reshape(key_count, HEADS, HEAD_DIM)
    v_heads = values.astype(jnp.float32).reshape(key_count, HEADS, HEAD_DIM)
    scores = jnp.einsum("rhd,shd->rhs", q_heads, k_heads) * (HEAD_DIM ** -0.5)
    highest = jnp.max(scores, axis=-1, keepdims=True)
    powers = jnp.exp(scores - highest)
    totals = jnp.sum(powers, axis=-1)
    weights = lax.optimization_barrier(powers.astype(jnp.bfloat16)).astype(jnp.float32)
    summed = jnp.einsum("rhs,shd->rhd", weights, v_heads)
    return summed / totals[..., None]


def reference(img_q, img_kv, stale_mant, stale_exp, txt_q, txt_kv, order, timestep, gate_table):
    width = HEADS * HEAD_DIM
    row_index = jnp.arange(IMG, dtype=jnp.int32)
    owner = row_index // TOK_DEV
    position = (order[owner] * TOK_DEV + row_index % TOK_DEV).astype(jnp.float32)
    q_turned = rotate_rows(img_q, position)
    k_turned = rotate_rows(img_kv[0], position)
    fresh_values = img_kv[1]
    scaling = jnp.exp2(stale_exp.astype(jnp.float32))
    stale = (stale_mant.astype(jnp.float32).reshape(2, IMG, HEADS, HEAD_DIM) * scaling[..., None]).reshape(2, IMG, width).astype(jnp.bfloat16)

    def image_block(device):
        queries = lax.dynamic_slice_in_dim(q_turned, device * TOK_DEV, TOK_DEV, 0)
        mine = (owner == device)[:, None]
        keys = jnp.where(mine, k_turned, stale[0])
        values = jnp.where(mine, fresh_values, stale[1])
        return attend(queries, jnp.concatenate([txt_kv[0], keys], axis=0), jnp.concatenate([txt_kv[1], values], axis=0))

    image_heads = lax.map(image_block, jnp.arange(PATCHES, dtype=jnp.int32)).reshape(IMG, width)
    gate = gate_table[timestep[0]]
    img_out = (gate[0] * image_heads).astype(jnp.bfloat16)
    text_heads = attend(txt_q, jnp.concatenate([txt_kv[0], k_turned], axis=0), jnp.concatenate([txt_kv[1], fresh_values], axis=0)).reshape(TXT, width)
    txt_out = (gate[1] * text_heads).astype(jnp.bfloat16)
    return img_out, txt_out
```

```python
import functools
import math

import jax
import jax.numpy as jnp
from jax import lax
from jax.experimental import pallas as pl
from jax.experimental.pallas import tpu as pltpu
from jax.sharding import PartitionSpec as P

VMEM = pl.BlockSpec(memory_space=pltpu.VMEM)
SMEM = pl.BlockSpec(memory_space=pltpu.SMEM)
NT = (((1,), (1,)), ((), ()))
LOG2E = 1.4426950408889634


def turn_tables(first, rows, head_dim):
    half = head_dim // 2
    lane = lax.broadcasted_iota(jnp.int32, (rows, head_dim), 1)
    row = lax.broadcasted_iota(jnp.int32, (rows, head_dim), 0)
    low = lane < half
    index = jnp.where(low, lane, lane - half).astype(jnp.float32)
    frequency = jnp.exp(index * (-math.log(10000.0) / half))
    angles = (first + row).astype(jnp.float32) * frequency
    sine = jnp.sin(angles)
    return jnp.cos(angles), jnp.where(low, -sine, sine)


def turn(x, cosine, sine):
    return x * cosine + pltpu.roll(x, x.shape[1] // 2, axis=1) * sine


def pack_kernel(order_ref, kv_ref, mant_ref, exp_ref, block_ref):
    rows, width = kv_ref.shape[1:]
    heads = exp_ref.shape[2]
    head_dim = width // heads
    cosine, sine = turn_tables(order_ref[0] * rows, rows, head_dim)
    for which in range(2):
        power = jnp.exp2(exp_ref[which].astype(jnp.float32))
        power = power.astype(jnp.bfloat16).astype(jnp.float32)
        for head in range(heads):
            span = slice(head * head_dim, (head + 1) * head_dim)
            fresh = kv_ref[which, :, span].astype(jnp.float32)
            if which == 0:
                fresh = turn(fresh, cosine, sine)
            stale = mant_ref[which, :, span].astype(jnp.float32) * power[:, head : head + 1]
            both = jnp.concatenate([fresh, stale], axis=0).astype(jnp.bfloat16)
            start = which * width + head * head_dim
            block_ref[:, start : start + head_dim] = both


def attend(queries, keys, values, scale):
    scores = lax.dot_general(queries, keys, NT, preferred_element_type=jnp.float32)
    highest = jnp.max(scores, axis=-1, keepdims=True)
    powers = jnp.exp2((scores - highest) * scale)
    totals = jnp.sum(powers, axis=-1, keepdims=True)
    summed = jnp.dot(powers.astype(jnp.bfloat16), values, preferred_element_type=jnp.float32)
    return summed / totals


def attend_kernel(heads, rows, order_ref, time_ref, gate_ref, q_ref, txt_q_ref, txt_kv_ref, *refs):
    blocks, (img_out_ref, txt_out_ref) = refs[:-2], refs[-2:]
    width = q_ref.shape[1]
    head_dim = width // heads
    scale = head_dim ** (-0.5) * LOG2E
    cosine, sine = turn_tables(order_ref[0] * rows, rows, head_dim)
    for head in range(heads):
        span = slice(head * head_dim, (head + 1) * head_dim)
        parts = []
        for which in range(2):
            start = which * width + head * head_dim
            fresh, stale = [], []
            for number, block in enumerate(blocks):
                for place in range(block.shape[0]):
                    both = block[place, :, start : start + head_dim].astype(jnp.float32)
                    own = number == 0 and place == 0
                    fresh.append(both[:rows])
                    stale.append(both[:rows] if own else both[rows:])
            parts.append([jnp.concatenate(p, axis=0).astype(jnp.bfloat16) for p in (fresh, stale)])
        (new_keys, old_keys), (new_values, old_values) = parts
        txt_keys, txt_values = txt_kv_ref[0, :, span], txt_kv_ref[1, :, span]
        text = attend(
            txt_q_ref[:, span],
            jnp.concatenate([txt_keys, new_keys], axis=0),
            jnp.concatenate([txt_values, new_values], axis=0),
            scale,
        )
        txt_out_ref[:, span] = (text * gate_ref[0, 1:2, span]).astype(jnp.bfloat16)
        queries = turn(q_ref[:, span].astype(jnp.float32), cosine, sine).astype(jnp.bfloat16)
        image = attend(
            queries,
            jnp.concatenate([txt_keys, old_keys], axis=0),
            jnp.concatenate([txt_values, old_values], axis=0),
            scale,
        )
        img_out_ref[:, span] = (image * gate_ref[0, 0:1, span]).astype(jnp.bfloat16)


def swap(x, even, odd=None):
    odd = even if odd is None else odd
    count = lax.axis_size("patch")
    pairs = [(i, i ^ (odd if i % 2 else even)) for i in range(count)]
    return lax.ppermute(x, "patch", pairs)


def gather_blocks(block):
    count = lax.axis_size("patch")
    block = block[None]
    if count == 16:
        hops = ((2, 8), (8, 4), (4, 2))
        one, two, three = (swap(block, *hop) for hop in hops)
        one_two = swap(one, *hops[1])
        one_three = swap(one, *hops[2])
        two_three = swap(two, *hops[2])
        all_three = swap(one_two, *hops[2])
        blocks = [block, one, two, three, one_two, one_three, two_three, all_three]
        return blocks + [swap(b, 1) for b in blocks]
    if count & (count - 1) == 0:
        bit = count // 2
        while bit:
            block = jnp.concatenate([block, swap(block, bit)], axis=0)
            bit //= 2
        return [block]
    blocks = [block]
    ring = [(i, (i + 1) % count) for i in range(count)]
    for _ in range(count - 1):
        blocks.append(lax.ppermute(blocks[-1], "patch", ring))
    return blocks


def on_device(img_q, img_kv, stale_mant, stale_exp, txt_q, txt_kv, order, timestep, gate_table):
    rows, width = img_q.shape
    heads = stale_exp.shape[2]
    block = pl.pallas_call(
        pack_kernel,
        out_shape=jax.ShapeDtypeStruct((2 * rows, 2 * width), jnp.bfloat16),
        in_specs=[SMEM, VMEM, VMEM, VMEM],
        out_specs=VMEM,
        name="pack",
    )(order, img_kv, stale_mant, stale_exp)
    blocks = gather_blocks(block)
    gate = lax.dynamic_index_in_dim(gate_table, timestep[0], 0, keepdims=True)
    return pl.pallas_call(
        functools.partial(attend_kernel, heads, rows),
        out_shape=(
            jax.ShapeDtypeStruct(img_q.shape, jnp.bfloat16),
            jax.ShapeDtypeStruct(txt_q.shape, jnp.bfloat16),
        ),
        in_specs=[SMEM, SMEM] + [VMEM] * (4 + len(blocks)),
        out_specs=(VMEM, VMEM),
        compiler_params=pltpu.CompilerParams(vmem_limit_bytes=40 << 20),
        name="attend",
    )(order, timestep, gate, img_q, txt_q, txt_kv, *blocks)


def solution(mesh):
    in_specs = (
        P(("groups", "patch"), None),
        P(None, ("groups", "patch"), None),
        P(None, ("groups", "patch"), None),
        P(None, ("groups", "patch"), None),
        P("groups", None),
        P(None, "groups", None),
        P(("groups", "patch")),
        P("groups"),
        P(),
    )
    out_specs = (P(("groups", "patch"), None), P("groups", None))
    return jax.shard_map(
        on_device, mesh=mesh, in_specs=in_specs, out_specs=out_specs, check_vma=False
    )
```

```python
import functools
import math

import jax
import jax.numpy as jnp
from jax import lax
from jax.experimental import pallas as pl
from jax.experimental.pallas import tpu as pltpu
from jax.sharding import PartitionSpec as P

VMEM = pl.BlockSpec(memory_space=pltpu.VMEM)
HBM = pl.BlockSpec(memory_space=pltpu.HBM)
SMEM = pl.BlockSpec(memory_space=pltpu.SMEM)
NT = (((1,), (1,)), ((), ()))
LOG2E = 1.4426950408889634
HIDDEN = -1e30
HOPS = ((2, 8), (8, 4), (4, 2))


def turn_tables(first, rows, head_dim):
    half = head_dim // 2
    lane = lax.broadcasted_iota(jnp.int32, (rows, head_dim), 1)
    row = lax.broadcasted_iota(jnp.int32, (rows, head_dim), 0)
    low = lane < half
    index = jnp.where(low, lane, lane - half).astype(jnp.float32)
    frequency = jnp.exp(index * (-math.log(10000.0) / half))
    angles = (first + row).astype(jnp.float32) * frequency
    sine = jnp.sin(angles)
    return jnp.cos(angles), jnp.where(low, -sine, sine)


def turn(x, cosine, sine):
    return x * cosine + pltpu.roll(x, x.shape[1] // 2, axis=1) * sine


def pack_kernel(order_ref, kv_hbm, mant_hbm, exp_hbm, block_ref, kv, mant, exp, sems):
    copies = [
        pltpu.make_async_copy(source, target, sems.at[i])
        for i, (source, target) in enumerate(((exp_hbm, exp), (kv_hbm, kv), (mant_hbm, mant)))
    ]
    for copy in copies:
        copy.start()
    rows, width = kv.shape[1:]
    heads = exp.shape[2]
    head_dim = width // heads
    cosine, sine = turn_tables(order_ref[...] * rows, rows, head_dim)
    for copy in copies:
        copy.wait()
    for which in range(2):
        power = jnp.exp2(exp[which].astype(jnp.float32))
        power = power.astype(jnp.bfloat16).astype(jnp.float32)
        for head in range(heads):
            span = slice(head * head_dim, (head + 1) * head_dim)
            fresh = kv[which, :, span].astype(jnp.float32)
            if which == 0:
                fresh = turn(fresh, cosine, sine)
            stale = mant[which, :, span].astype(jnp.float32) * power[:, head : head + 1]
            both = jnp.concatenate([fresh, stale], axis=0).astype(jnp.bfloat16)
            start = which * width + head * head_dim
            block_ref[:, start : start + head_dim] = both


def join_copies(blocks, joined_ref, sems):
    copies = []
    place = 0
    for i, block in enumerate(blocks):
        span = pl.ds(place, block.shape[0])
        copies.append(pltpu.make_async_copy(block, joined_ref.at[span], sems.at[i]))
        place += block.shape[0]
    return copies


def with_ones(values):
    return jnp.concatenate([values, jnp.ones_like(values)], axis=1)


def text_kernel(heads, count, *refs):
    order_ref, q_hbm, txt_q_hbm, txt_kv_hbm = refs[:4]
    blocks = refs[4 : 4 + count]
    joined_ref, txt_q, turned_ref, mean_ref, level_ref = refs[4 + count : 9 + count]
    q, txt_kv, powers_ref, sems, join_sems = refs[9 + count :]
    q_copy = pltpu.make_async_copy(q_hbm, q, sems.at[0])
    txt_q_copy = pltpu.make_async_copy(txt_q_hbm, txt_q, sems.at[1])
    keys_copy = pltpu.make_async_copy(txt_kv_hbm.at[0], txt_kv.at[0], sems.at[2])
    values_copy = pltpu.make_async_copy(txt_kv_hbm.at[1], txt_kv.at[1], sems.at[3])
    joins = join_copies(blocks, joined_ref, join_sems)
    for copy in [q_copy, txt_q_copy, keys_copy, values_copy] + joins:
        copy.start()
    rows, width = q.shape
    head_dim = width // heads
    scale = head_dim ** (-0.5) * LOG2E
    cosine, sine = turn_tables(order_ref[...] * rows, rows, head_dim)
    q_copy.wait()
    for head in range(heads):
        span = slice(head * head_dim, (head + 1) * head_dim)
        turned = turn(q[:, span].astype(jnp.float32), cosine, sine)
        turned_ref[:, span] = turned.astype(jnp.bfloat16)
    txt_q_copy.wait()
    keys_copy.wait()
    for head in range(heads):
        span = slice(head * head_dim, (head + 1) * head_dim)
        queries = jnp.concatenate([txt_q[:, span], turned_ref[:, span]], axis=0)
        scores = lax.dot_general(queries, txt_kv[0, :, span], NT, preferred_element_type=jnp.float32)
        scores = scores * scale
        highest = jnp.max(scores, axis=-1, keepdims=True)
        powers_ref[head] = jnp.exp2(scores - highest).astype(jnp.bfloat16)
        level_ref[:, span] = jnp.broadcast_to(highest, (highest.shape[0], head_dim))
    values_copy.wait()
    for head in range(heads):
        span = slice(head * head_dim, (head + 1) * head_dim)
        summed = jnp.dot(
            powers_ref[head], with_ones(txt_kv[1, :, span]), preferred_element_type=jnp.float32
        )
        mean_ref[:, span] = summed[:, :head_dim] / summed[:, head_dim:]
        level_ref[:, span] = level_ref[:, span] + jnp.log2(summed[:, head_dim:])
    for copy in joins:
        copy.wait()


def image_kernel(heads, time_ref, gate_hbm, txt_q_ref, turned_ref, mean_ref, level_ref, *refs):
    blocks = refs[:-5]
    img_out_ref, txt_out_ref, gate, held, gate_sem = refs[-5:]
    gate_copy = pltpu.make_async_copy(gate_hbm.at[time_ref[0]], gate, gate_sem)
    gate_copy.start()
    rows, width = img_out_ref.shape
    head_dim = width // heads
    text_rows = txt_q_ref.shape[0]
    scale = head_dim ** (-0.5) * LOG2E
    columns = 2 * rows * sum(block.shape[0] for block in blocks)
    column = lax.broadcasted_iota(jnp.int32, (rows, columns), 1)
    fresh = lax.rem(column, 2 * rows) < rows
    no_stale = jnp.where(fresh, 0.0, HIDDEN)
    no_fresh = jnp.where(fresh, HIDDEN, 0.0)
    image_mask = jnp.where(column < 2 * rows, no_stale, no_fresh)
    text_mask = jnp.broadcast_to(no_stale[:1], (text_rows, columns))
    mask = jnp.concatenate([text_mask, image_mask], axis=0)
    def store(head, result):
        span = slice(head * head_dim, (head + 1) * head_dim)
        txt_out_ref[:, span] = (result[:text_rows] * gate[1:2, span]).astype(jnp.bfloat16)
        img_out_ref[:, span] = (result[text_rows:] * gate[0:1, span]).astype(jnp.bfloat16)

    waiting = held.shape[0]
    for head in range(heads):
        span = slice(head * head_dim, (head + 1) * head_dim)
        keys, values = (
            jnp.concatenate(
                [
                    block[i, :, start : start + head_dim]
                    for block in blocks
                    for i in range(block.shape[0])
                ],
                axis=0,
            )
            for start in (head * head_dim, width + head * head_dim)
        )
        queries = jnp.concatenate([txt_q_ref[:, span], turned_ref[:, span]], axis=0)
        scores = lax.dot_general(queries, keys, NT, preferred_element_type=jnp.float32)
        scores = scores * scale + mask
        level = level_ref[:, span]
        highest = jnp.maximum(level, jnp.max(scores, axis=-1, keepdims=True))
        weight = jnp.exp2(level - highest)
        powers = jnp.exp2(scores - jnp.concatenate([highest] * (columns // head_dim), axis=1))
        summed = jnp.dot(
            powers.astype(jnp.bfloat16), with_ones(values), preferred_element_type=jnp.float32
        )
        result = (mean_ref[:, span] * weight + summed[:, :head_dim]) / (weight + summed[:, head_dim:])
        if head < waiting:
            held[head] = result
            if head == waiting - 1:
                gate_copy.wait()
                for early in range(waiting):
                    store(early, held[early])
        else:
            store(head, result)


def swap(x, even, odd=None):
    odd = even if odd is None else odd
    count = lax.axis_size("patch")
    pairs = [(i, i ^ (odd if i % 2 else even)) for i in range(count)]
    return lax.ppermute(x, "patch", pairs)


def gather_columns(block):
    count = lax.axis_size("patch")
    block = block[None]
    if count == 16:
        hops = HOPS
        one = swap(block, *hops[0])
        three = swap(block, *hops[2])
        one_two = swap(one, *hops[1])
        two = swap(block, *hops[1])
        one_three = swap(one, *hops[2])
        two_three = swap(two, *hops[2])
        all_three = swap(one_two, *hops[2])
        return [block, one, two, three, one_two], [one_three, two_three, all_three]
    if count & (count - 1) == 0:
        bit = count // 2
        while bit:
            block = jnp.concatenate([block, swap(block, bit)], axis=0)
            bit //= 2
        return [block], []
    blocks = [block]
    ring = [(i, (i + 1) % count) for i in range(count)]
    for _ in range(count - 1):
        blocks.append(lax.ppermute(blocks[-1], "patch", ring))
    return blocks, []


def on_device(img_q, img_kv, stale_mant, stale_exp, txt_q, txt_kv, order, timestep, gate_table):
    rows, width = img_q.shape
    heads = stale_exp.shape[2]
    text_rows = txt_q.shape[0]
    all_rows = text_rows + rows
    bf16, f32 = jnp.bfloat16, jnp.float32
    img_q, img_kv, stale_mant, stale_exp, gate_table, txt_q, txt_kv = (
        pltpu.with_memory_space_constraint(x, pltpu.HBM)
        for x in (img_q, img_kv, stale_mant, stale_exp, gate_table, txt_q, txt_kv)
    )
    order = order.reshape(1, 1)
    block = pl.pallas_call(
        pack_kernel,
        out_shape=pltpu.VMEM((2 * rows, 2 * width), bf16),
        in_specs=[VMEM] + [HBM] * 3,
        out_specs=VMEM,
        scratch_shapes=[
            pltpu.VMEM(img_kv.shape, img_kv.dtype),
            pltpu.VMEM(stale_mant.shape, stale_mant.dtype),
            pltpu.VMEM(stale_exp.shape, stale_exp.dtype),
            pltpu.SemaphoreType.DMA((3,)),
        ],
        name="pack",
    )(order, img_kv, stale_mant, stale_exp)
    early, late = gather_columns(block)
    joined = sum(x.shape[0] for x in early)
    first, *states = pl.pallas_call(
        functools.partial(text_kernel, heads, len(early)),
        out_shape=(
            pltpu.VMEM((joined,) + block.shape, bf16),
            pltpu.VMEM(txt_q.shape, bf16),
            pltpu.VMEM((rows, width), bf16),
            pltpu.VMEM((all_rows, width), f32),
            pltpu.VMEM((all_rows, width), f32),
        ),
        in_specs=[VMEM] + [HBM] * 3 + [VMEM] * len(early),
        out_specs=[VMEM] * 5,
        scratch_shapes=[
            pltpu.VMEM(img_q.shape, img_q.dtype),
            pltpu.VMEM(txt_kv.shape, txt_kv.dtype),
            pltpu.VMEM((heads, all_rows, text_rows), bf16),
            pltpu.SemaphoreType.DMA((4,)),
            pltpu.SemaphoreType.DMA((len(early),)),
        ],
        compiler_params=pltpu.CompilerParams(vmem_limit_bytes=16 << 20),
        name="text",
    )(order, img_q, txt_q, txt_kv, *early)
    blocks = [first] + late
    if lax.axis_size("patch") == 16:
        blocks = list(lax.optimization_barrier(tuple(blocks)))
        blocks += [swap(x, 1) for x in blocks]
    return pl.pallas_call(
        functools.partial(image_kernel, heads),
        out_shape=(
            jax.ShapeDtypeStruct(img_q.shape, bf16),
            jax.ShapeDtypeStruct(txt_q.shape, bf16),
        ),
        in_specs=[SMEM, HBM] + [VMEM] * (len(states) + len(blocks)),
        out_specs=(VMEM, VMEM),
        scratch_shapes=[
            pltpu.VMEM(gate_table.shape[1:], f32),
            pltpu.VMEM((6, all_rows, width // heads), f32),
            pltpu.SemaphoreType.DMA,
        ],
        compiler_params=pltpu.CompilerParams(vmem_limit_bytes=32 << 20),
        name="image",
    )(timestep, gate_table, *states, *blocks)


def solution(mesh):
    in_specs = (
        P(("groups", "patch"), None),
        P(None, ("groups", "patch"), None),
        P(None, ("groups", "patch"), None),
        P(None, ("groups", "patch"), None),
        P("groups", None),
        P(None, "groups", None),
        P(("groups", "patch")),
        P("groups"),
        P(),
    )
    out_specs = (P(("groups", "patch"), None), P("groups", None))
    return jax.shard_map(
        on_device, mesh=mesh, in_specs=in_specs, out_specs=out_specs, check_vma=False
    )
```

```python
import functools
import math

import jax
import jax.numpy as jnp
from jax import lax
from jax.experimental import pallas as pl
from jax.experimental.pallas import tpu as pltpu
from jax.sharding import PartitionSpec as P

VMEM = pl.BlockSpec(memory_space=pltpu.VMEM)
HBM = pl.BlockSpec(memory_space=pltpu.HBM)
SMEM = pl.BlockSpec(memory_space=pltpu.SMEM)
NT = (((1,), (1,)), ((), ()))
LOG2E = 1.4426950408889634
HIDDEN = -1e30
HOPS = ((2, 12), (8, 4), (4, 2))


def turn_tables(first, rows, head_dim):
    half = head_dim // 2
    lane = lax.broadcasted_iota(jnp.int32, (rows, head_dim), 1)
    row = lax.broadcasted_iota(jnp.int32, (rows, head_dim), 0)
    low = lane < half
    index = jnp.where(low, lane, lane - half).astype(jnp.float32)
    frequency = jnp.exp(index * (-math.log(10000.0) / half))
    angles = (first + row).astype(jnp.float32) * frequency
    sine = jnp.sin(angles)
    return jnp.cos(angles), jnp.where(low, -sine, sine)


def turn(x, cosine, sine):
    return x * cosine + pltpu.roll(x, x.shape[1] // 2, axis=1) * sine


def pack_kernel(order_ref, kv_hbm, mant_hbm, exp_hbm, block_ref, kv, mant, exp, sems):
    copies = [
        pltpu.make_async_copy(source, target, sems.at[i])
        for i, (source, target) in enumerate(((exp_hbm, exp), (kv_hbm, kv), (mant_hbm, mant)))
    ]
    for copy in copies:
        copy.start()
    rows, width = kv.shape[1:]
    heads = exp.shape[2]
    head_dim = width // heads
    cosine, sine = turn_tables(order_ref[...] * rows, rows, head_dim)
    for copy in copies:
        copy.wait()
    for which in range(2):
        power = jnp.exp2(exp[which].astype(jnp.float32))
        power = power.astype(jnp.bfloat16).astype(jnp.float32)
        for head in range(heads):
            span = slice(head * head_dim, (head + 1) * head_dim)
            fresh = kv[which, :, span].astype(jnp.float32)
            if which == 0:
                fresh = turn(fresh, cosine, sine)
            stale = mant[which, :, span].astype(jnp.float32) * power[:, head : head + 1]
            both = jnp.concatenate([fresh, stale], axis=0).astype(jnp.bfloat16)
            start = which * width + head * head_dim
            block_ref[:, start : start + head_dim] = both


def join_kernel(*refs):
    for i, block in enumerate(refs[:-1]):
        refs[-1][i] = block[0]


def join(*blocks):
    return pl.pallas_call(
        join_kernel,
        out_shape=pltpu.VMEM((len(blocks),) + blocks[0].shape[1:], blocks[0].dtype),
        in_specs=[VMEM] * len(blocks),
        out_specs=VMEM,
        compiler_params=pltpu.CompilerParams(vmem_limit_bytes=2 << 20),
        name="join",
    )(*blocks)


def with_ones(values):
    return jnp.concatenate([values, jnp.ones_like(values)], axis=1)


def text_first_kernel(heads, share, order_ref, q_hbm, txt_q_hbm, txt_kv_hbm, gate_hbm, *refs):
    gate_ref, txt_q, txt_kv, turned_ref, mean_ref, level_ref, q, powers_ref, sems = refs
    q_copy = pltpu.make_async_copy(q_hbm, q, sems.at[0])
    txt_q_copy = pltpu.make_async_copy(txt_q_hbm, txt_q, sems.at[1])
    keys_copy = pltpu.make_async_copy(txt_kv_hbm.at[0], txt_kv.at[0], sems.at[2])
    values_copy = pltpu.make_async_copy(txt_kv_hbm.at[1], txt_kv.at[1], sems.at[3])
    gate_copy = pltpu.make_async_copy(gate_hbm, gate_ref, sems.at[4])
    for copy in (q_copy, txt_q_copy, keys_copy, values_copy, gate_copy):
        copy.start()
    rows, width = q.shape
    head_dim = width // heads
    scale = head_dim ** (-0.5) * LOG2E
    cosine, sine = turn_tables(order_ref[...] * rows, rows, head_dim)
    q_copy.wait()
    for head in range(heads):
        span = slice(head * head_dim, (head + 1) * head_dim)
        turned = turn(q[:, span].astype(jnp.float32), cosine, sine)
        turned_ref[:, span] = turned.astype(jnp.bfloat16)
    txt_q_copy.wait()
    keys_copy.wait()
    for head in range(share):
        span = slice(head * head_dim, (head + 1) * head_dim)
        queries = jnp.concatenate([txt_q[:, span], turned_ref[:, span]], axis=0)
        scores = lax.dot_general(queries, txt_kv[0, :, span], NT, preferred_element_type=jnp.float32)
        scores = scores * scale
        highest = jnp.max(scores, axis=-1, keepdims=True)
        powers_ref[head] = jnp.exp2(scores - highest).astype(jnp.bfloat16)
        level_ref[:, span] = jnp.broadcast_to(highest, (highest.shape[0], head_dim))
    values_copy.wait()
    for head in range(share):
        span = slice(head * head_dim, (head + 1) * head_dim)
        summed = jnp.dot(
            powers_ref[head], with_ones(txt_kv[1, :, span]), preferred_element_type=jnp.float32
        )
        mean_ref[:, span] = summed[:, :head_dim] / summed[:, head_dim:]
        level_ref[:, span] = level_ref[:, span] + jnp.log2(summed[:, head_dim:])
    gate_copy.wait()


def text_second_kernel(heads, first, txt_q, txt_kv, turned_ref, mean_ref, level_ref):
    head_dim = txt_q.shape[1] // heads
    scale = head_dim ** (-0.5) * LOG2E
    for head in range(first, heads):
        span = slice(head * head_dim, (head + 1) * head_dim)
        here = slice((head - first) * head_dim, (head - first + 1) * head_dim)
        queries = jnp.concatenate([txt_q[:, span], turned_ref[:, span]], axis=0)
        scores = lax.dot_general(queries, txt_kv[0, :, span], NT, preferred_element_type=jnp.float32)
        scores = scores * scale
        highest = jnp.max(scores, axis=-1, keepdims=True)
        powers = jnp.exp2(scores - highest).astype(jnp.bfloat16)
        summed = jnp.dot(powers, with_ones(txt_kv[1, :, span]), preferred_element_type=jnp.float32)
        mean_ref[:, here] = summed[:, :head_dim] / summed[:, head_dim:]
        level_ref[:, here] = highest + jnp.log2(summed[:, head_dim:])


def image_kernel(heads, first, time_ref, gate_ref, txt_q_ref, turned_ref, *refs):
    states, blocks, (img_out_ref, txt_out_ref) = refs[:4], refs[4:-2], refs[-2:]
    time = time_ref[0]
    rows, width = img_out_ref.shape
    head_dim = width // heads
    text_rows = txt_q_ref.shape[0]
    scale = head_dim ** (-0.5) * LOG2E
    columns = 2 * rows * sum(block.shape[0] for block in blocks)
    column = lax.broadcasted_iota(jnp.int32, (rows, columns), 1)
    fresh = lax.rem(column, 2 * rows) < rows
    no_stale = jnp.where(fresh, 0.0, HIDDEN)
    no_fresh = jnp.where(fresh, HIDDEN, 0.0)
    image_mask = jnp.where(column < 2 * rows, no_stale, no_fresh)
    text_mask = jnp.broadcast_to(no_stale[:1], (text_rows, columns))
    mask = jnp.concatenate([text_mask, image_mask], axis=0)
    for head in range(heads):
        span = slice(head * head_dim, (head + 1) * head_dim)
        mean_ref, level_ref = states[:2] if head < first else states[2:]
        place = head if head < first else head - first
        here = slice(place * head_dim, (place + 1) * head_dim)
        keys, values = (
            jnp.concatenate(
                [
                    block[i, :, start : start + head_dim]
                    for block in blocks
                    for i in range(block.shape[0])
                ],
                axis=0,
            )
            for start in (head * head_dim, width + head * head_dim)
        )
        queries = jnp.concatenate([txt_q_ref[:, span], turned_ref[:, span]], axis=0)
        scores = lax.dot_general(queries, keys, NT, preferred_element_type=jnp.float32)
        scores = scores * scale + mask
        level = level_ref[:, here]
        highest = jnp.maximum(level, jnp.max(scores, axis=-1, keepdims=True))
        weight = jnp.exp2(level - highest)
        powers = jnp.exp2(scores - jnp.concatenate([highest] * (columns // head_dim), axis=1))
        summed = jnp.dot(
            powers.astype(jnp.bfloat16), with_ones(values), preferred_element_type=jnp.float32
        )
        result = (mean_ref[:, here] * weight + summed[:, :head_dim]) / (weight + summed[:, head_dim:])
        gate = gate_ref[time, :, span]
        txt_out_ref[:, span] = (result[:text_rows] * gate[1:2]).astype(jnp.bfloat16)
        img_out_ref[:, span] = (result[text_rows:] * gate[0:1]).astype(jnp.bfloat16)


def swap(x, even, odd=None):
    odd = even if odd is None else odd
    count = lax.axis_size("patch")
    pairs = [(i, i ^ (odd if i % 2 else even)) for i in range(count)]
    return lax.ppermute(x, "patch", pairs)


def gather_blocks(block):
    count = lax.axis_size("patch")
    if count == 16:
        one, two, three = (swap(block, *hop) for hop in HOPS)
        one_two = swap(one, *HOPS[1])
        one_three = swap(one, *HOPS[2])
        two_three = swap(two, *HOPS[2])
        all_three = swap(one_two, *HOPS[2])
        return [block, one, two, three], [one_two, one_three, two_three, all_three]
    if count & (count - 1) == 0:
        bit = count // 2
        while bit:
            block = jnp.concatenate([block, swap(block, bit)], axis=0)
            bit //= 2
        return [block], []
    blocks = [block]
    ring = [(i, (i + 1) % count) for i in range(count)]
    for _ in range(count - 1):
        blocks.append(lax.ppermute(blocks[-1], "patch", ring))
    return blocks, []


def on_device(img_q, img_kv, stale_mant, stale_exp, txt_q, txt_kv, order, timestep, gate_table):
    rows, width = img_q.shape
    heads = stale_exp.shape[2]
    text_rows = txt_q.shape[0]
    all_rows = text_rows + rows
    bf16, f32 = jnp.bfloat16, jnp.float32
    img_q, img_kv, stale_mant, stale_exp, gate_table, txt_q, txt_kv = (
        pltpu.with_memory_space_constraint(x, pltpu.HBM)
        for x in (img_q, img_kv, stale_mant, stale_exp, gate_table, txt_q, txt_kv)
    )
    order = order.reshape(1, 1)
    block = pl.pallas_call(
        pack_kernel,
        out_shape=pltpu.VMEM((2 * rows, 2 * width), bf16),
        in_specs=[VMEM] + [HBM] * 3,
        out_specs=VMEM,
        scratch_shapes=[
            pltpu.VMEM(img_kv.shape, img_kv.dtype),
            pltpu.VMEM(stale_mant.shape, stale_mant.dtype),
            pltpu.VMEM(stale_exp.shape, stale_exp.dtype),
            pltpu.SemaphoreType.DMA((3,)),
        ],
        compiler_params=pltpu.CompilerParams(vmem_limit_bytes=4 << 20),
        name="pack",
    )(order, img_kv, stale_mant, stale_exp)
    blocks, late = gather_blocks(block[None])
    if late:
        near = join(*blocks)
        near, order = lax.optimization_barrier((near, order))
        blocks = [near]
    share = 2 * heads // 3
    part = share * (width // heads)
    gate, txt_q, txt_kv, turned, *state = pl.pallas_call(
        functools.partial(text_first_kernel, heads, share),
        out_shape=(
            pltpu.VMEM(gate_table.shape, f32),
            pltpu.VMEM(txt_q.shape, bf16),
            pltpu.VMEM(txt_kv.shape, bf16),
            pltpu.VMEM((rows, width), bf16),
            pltpu.VMEM((all_rows, part), f32),
            pltpu.VMEM((all_rows, part), f32),
        ),
        in_specs=[VMEM] + [HBM] * 4,
        out_specs=[VMEM] * 6,
        scratch_shapes=[
            pltpu.VMEM(img_q.shape, img_q.dtype),
            pltpu.VMEM((share, all_rows, text_rows), bf16),
            pltpu.SemaphoreType.DMA((5,)),
        ],
        compiler_params=pltpu.CompilerParams(vmem_limit_bytes=16 << 20),
        name="text_first",
    )(order, img_q, txt_q, txt_kv, gate_table)
    if late:
        near, gate, txt_q, txt_kv, turned, *state = lax.optimization_barrier(
            (near, gate, txt_q, txt_kv, turned, *state)
        )
        blocks = [near, swap(near, 1)]
    rest = pl.pallas_call(
        functools.partial(text_second_kernel, heads, share),
        out_shape=(
            pltpu.VMEM((all_rows, width - part), f32),
            pltpu.VMEM((all_rows, width - part), f32),
        ),
        in_specs=[VMEM] * 3,
        out_specs=[VMEM] * 2,
        compiler_params=pltpu.CompilerParams(vmem_limit_bytes=16 << 20),
        name="text_second",
    )(txt_q, txt_kv, turned)
    states = (gate, txt_q, turned, *state, *rest)
    if late:
        far = join(*late)
        far, *states = lax.optimization_barrier((far, *states))
        blocks += [far, swap(far, 1)]
    return pl.pallas_call(
        functools.partial(image_kernel, heads, share),
        out_shape=(
            jax.ShapeDtypeStruct(img_q.shape, bf16),
            jax.ShapeDtypeStruct(txt_q.shape, bf16),
        ),
        in_specs=[SMEM] + [VMEM] * (len(states) + len(blocks)),
        out_specs=(VMEM, VMEM),
        compiler_params=pltpu.CompilerParams(vmem_limit_bytes=32 << 20),
        name="image",
    )(timestep, *states, *blocks)


def solution(mesh):
    in_specs = (
        P(("groups", "patch"), None),
        P(None, ("groups", "patch"), None),
        P(None, ("groups", "patch"), None),
        P(None, ("groups", "patch"), None),
        P("groups", None),
        P(None, "groups", None),
        P(("groups", "patch")),
        P("groups"),
        P(),
    )
    out_specs = (P(("groups", "patch"), None), P("groups", None))
    return jax.shard_map(
        on_device, mesh=mesh, in_specs=in_specs, out_specs=out_specs, check_vma=False
    )
```

```python
import functools
import math

import jax
import jax.numpy as jnp
from jax import lax
from jax.experimental import pallas as pl
from jax.experimental.pallas import tpu as pltpu
from jax.sharding import PartitionSpec as P

VMEM = pl.BlockSpec(memory_space=pltpu.VMEM)
HBM = pl.BlockSpec(memory_space=pltpu.HBM)
SMEM = pl.BlockSpec(memory_space=pltpu.SMEM)
NT = (((1,), (1,)), ((), ()))
LOG2E = 1.4426950408889634
HIDDEN = -1e30
HOPS = ((2, 12), (8, 4), (4, 2))


def turn_tables(first, rows, head_dim):
    half = head_dim // 2
    lane = lax.broadcasted_iota(jnp.int32, (rows, head_dim), 1)
    row = lax.broadcasted_iota(jnp.int32, (rows, head_dim), 0)
    low = lane < half
    index = jnp.where(low, lane, lane - half).astype(jnp.float32)
    frequency = jnp.exp(index * (-math.log(10000.0) / half))
    angles = (first + row).astype(jnp.float32) * frequency
    sine = jnp.sin(angles)
    return jnp.cos(angles), jnp.where(low, -sine, sine)


def turn(x, cosine, sine):
    return x * cosine + pltpu.roll(x, x.shape[1] // 2, axis=1) * sine


def pack_kernel(order_ref, kv_hbm, mant_hbm, exp_hbm, block_ref, kv, mant, exp, sems):
    copies = [
        pltpu.make_async_copy(source, target, sems.at[i])
        for i, (source, target) in enumerate(((exp_hbm, exp), (kv_hbm, kv), (mant_hbm, mant)))
    ]
    for copy in copies:
        copy.start()
    rows, width = kv.shape[1:]
    heads = exp.shape[2]
    head_dim = width // heads
    cosine, sine = turn_tables(order_ref[...] * rows, rows, head_dim)
    for copy in copies:
        copy.wait()
    for which in range(2):
        power = jnp.exp2(exp[which].astype(jnp.float32))
        power = power.astype(jnp.bfloat16).astype(jnp.float32)
        for head in range(heads):
            span = slice(head * head_dim, (head + 1) * head_dim)
            fresh = kv[which, :, span].astype(jnp.float32)
            if which == 0:
                fresh = turn(fresh, cosine, sine)
            stale = mant[which, :, span].astype(jnp.float32) * power[:, head : head + 1]
            both = jnp.concatenate([fresh, stale], axis=0).astype(jnp.bfloat16)
            start = which * width + head * head_dim
            block_ref[:, start : start + head_dim] = both


def join_kernel(count, *refs):
    for i, block in enumerate(refs[:count]):
        refs[-1][i] = block[0]


def join(blocks, after=()):
    return pl.pallas_call(
        functools.partial(join_kernel, len(blocks)),
        out_shape=pltpu.VMEM((len(blocks),) + blocks[0].shape[1:], blocks[0].dtype),
        in_specs=[VMEM] * (len(blocks) + len(after)),
        out_specs=VMEM,
        compiler_params=pltpu.CompilerParams(vmem_limit_bytes=2 << 20),
        name="join",
    )(*blocks, *after)


def with_ones(values):
    return jnp.concatenate([values, jnp.ones_like(values)], axis=1)


def text_first_kernel(heads, share, order_ref, q_hbm, txt_q_hbm, txt_kv_hbm, gate_hbm, *refs):
    gate_ref, txt_q, txt_kv, turned_ref, mean_ref, level_ref, q, powers_ref, sems = refs[-9:]
    q_copy = pltpu.make_async_copy(q_hbm, q, sems.at[0])
    txt_q_copy = pltpu.make_async_copy(txt_q_hbm, txt_q, sems.at[1])
    keys_copy = pltpu.make_async_copy(txt_kv_hbm.at[0], txt_kv.at[0], sems.at[2])
    values_copy = pltpu.make_async_copy(txt_kv_hbm.at[1], txt_kv.at[1], sems.at[3])
    gate_copy = pltpu.make_async_copy(gate_hbm, gate_ref, sems.at[4])
    for copy in (q_copy, txt_q_copy, keys_copy, values_copy, gate_copy):
        copy.start()
    rows, width = q.shape
    head_dim = width // heads
    scale = head_dim ** (-0.5) * LOG2E
    cosine, sine = turn_tables(order_ref[...] * rows, rows, head_dim)
    q_copy.wait()
    for head in range(heads):
        span = slice(head * head_dim, (head + 1) * head_dim)
        turned = turn(q[:, span].astype(jnp.float32), cosine, sine)
        turned_ref[:, span] = turned.astype(jnp.bfloat16)
    txt_q_copy.wait()
    keys_copy.wait()
    for head in range(share):
        span = slice(head * head_dim, (head + 1) * head_dim)
        queries = jnp.concatenate([txt_q[:, span], turned_ref[:, span]], axis=0)
        scores = lax.dot_general(queries, txt_kv[0, :, span], NT, preferred_element_type=jnp.float32)
        scores = scores * scale
        highest = jnp.max(scores, axis=-1, keepdims=True)
        powers_ref[head] = jnp.exp2(scores - highest).astype(jnp.bfloat16)
        level_ref[:, span] = jnp.broadcast_to(highest, (highest.shape[0], head_dim))
    values_copy.wait()
    for head in range(share):
        span = slice(head * head_dim, (head + 1) * head_dim)
        summed = jnp.dot(
            powers_ref[head], with_ones(txt_kv[1, :, span]), preferred_element_type=jnp.float32
        )
        mean_ref[:, span] = summed[:, :head_dim] / summed[:, head_dim:]
        level_ref[:, span] = level_ref[:, span] + jnp.log2(summed[:, head_dim:])
    gate_copy.wait()


def text_second_kernel(heads, first, txt_q, txt_kv, turned_ref, mean_ref, level_ref):
    head_dim = txt_q.shape[1] // heads
    scale = head_dim ** (-0.5) * LOG2E
    for head in range(first, heads):
        span = slice(head * head_dim, (head + 1) * head_dim)
        here = slice((head - first) * head_dim, (head - first + 1) * head_dim)
        queries = jnp.concatenate([txt_q[:, span], turned_ref[:, span]], axis=0)
        scores = lax.dot_general(queries, txt_kv[0, :, span], NT, preferred_element_type=jnp.float32)
        scores = scores * scale
        highest = jnp.max(scores, axis=-1, keepdims=True)
        powers = jnp.exp2(scores - highest).astype(jnp.bfloat16)
        summed = jnp.dot(powers, with_ones(txt_kv[1, :, span]), preferred_element_type=jnp.float32)
        mean_ref[:, here] = summed[:, :head_dim] / summed[:, head_dim:]
        level_ref[:, here] = highest + jnp.log2(summed[:, head_dim:])


def image_kernel(heads, first, time_ref, gate_ref, txt_q_ref, turned_ref, *refs):
    states, blocks, (img_out_ref, txt_out_ref) = refs[:4], refs[4:-2], refs[-2:]
    time = time_ref[0]
    rows, width = img_out_ref.shape
    head_dim = width // heads
    text_rows = txt_q_ref.shape[0]
    scale = head_dim ** (-0.5) * LOG2E
    columns = 2 * rows * sum(block.shape[0] for block in blocks)
    column = lax.broadcasted_iota(jnp.int32, (rows, columns), 1)
    fresh = lax.rem(column, 2 * rows) < rows
    no_stale = jnp.where(fresh, 0.0, HIDDEN)
    no_fresh = jnp.where(fresh, HIDDEN, 0.0)
    image_mask = jnp.where(column < 2 * rows, no_stale, no_fresh)
    text_mask = jnp.broadcast_to(no_stale[:1], (text_rows, columns))
    mask = jnp.concatenate([text_mask, image_mask], axis=0)
    for head in range(heads):
        span = slice(head * head_dim, (head + 1) * head_dim)
        mean_ref, level_ref = states[:2] if head < first else states[2:]
        place = head if head < first else head - first
        here = slice(place * head_dim, (place + 1) * head_dim)
        keys, values = (
            jnp.concatenate(
                [
                    block[i, :, start : start + head_dim]
                    for block in blocks
                    for i in range(block.shape[0])
                ],
                axis=0,
            )
            for start in (head * head_dim, width + head * head_dim)
        )
        queries = jnp.concatenate([txt_q_ref[:, span], turned_ref[:, span]], axis=0)
        scores = lax.dot_general(queries, keys, NT, preferred_element_type=jnp.float32)
        scores = scores * scale + mask
        level = level_ref[:, here]
        highest = jnp.maximum(level, jnp.max(scores, axis=-1, keepdims=True))
        weight = jnp.exp2(level - highest)
        powers = jnp.exp2(scores - jnp.concatenate([highest] * (columns // head_dim), axis=1))
        summed = jnp.dot(
            powers.astype(jnp.bfloat16), with_ones(values), preferred_element_type=jnp.float32
        )
        result = (mean_ref[:, here] * weight + summed[:, :head_dim]) / (weight + summed[:, head_dim:])
        gate = gate_ref[time, :, span]
        txt_out_ref[:, span] = (result[:text_rows] * gate[1:2]).astype(jnp.bfloat16)
        img_out_ref[:, span] = (result[text_rows:] * gate[0:1]).astype(jnp.bfloat16)


def swap(x, even, odd=None):
    odd = even if odd is None else odd
    count = lax.axis_size("patch")
    pairs = [(i, i ^ (odd if i % 2 else even)) for i in range(count)]
    return lax.ppermute(x, "patch", pairs)


def gather_blocks(block):
    count = lax.axis_size("patch")
    if count == 16:
        one, two, three = (swap(block, *hop) for hop in HOPS)
        one_two = swap(one, *HOPS[1])
        one_three = swap(one, *HOPS[2])
        two_three = swap(two, *HOPS[2])
        all_three = swap(one_two, *HOPS[2])
        return [block, one, two, three], [one_two, one_three, two_three, all_three]
    if count & (count - 1) == 0:
        bit = count // 2
        while bit:
            block = jnp.concatenate([block, swap(block, bit)], axis=0)
            bit //= 2
        return [block], []
    blocks = [block]
    ring = [(i, (i + 1) % count) for i in range(count)]
    for _ in range(count - 1):
        blocks.append(lax.ppermute(blocks[-1], "patch", ring))
    return blocks, []


def on_device(img_q, img_kv, stale_mant, stale_exp, txt_q, txt_kv, order, timestep, gate_table):
    rows, width = img_q.shape
    heads = stale_exp.shape[2]
    text_rows = txt_q.shape[0]
    all_rows = text_rows + rows
    bf16, f32 = jnp.bfloat16, jnp.float32
    img_q, img_kv, stale_mant, stale_exp, gate_table, txt_q, txt_kv = (
        pltpu.with_memory_space_constraint(x, pltpu.HBM)
        for x in (img_q, img_kv, stale_mant, stale_exp, gate_table, txt_q, txt_kv)
    )
    order = order.reshape(1, 1)
    block = pl.pallas_call(
        pack_kernel,
        out_shape=pltpu.VMEM((2 * rows, 2 * width), bf16),
        in_specs=[VMEM] + [HBM] * 3,
        out_specs=VMEM,
        scratch_shapes=[
            pltpu.VMEM(img_kv.shape, img_kv.dtype),
            pltpu.VMEM(stale_mant.shape, stale_mant.dtype),
            pltpu.VMEM(stale_exp.shape, stale_exp.dtype),
            pltpu.SemaphoreType.DMA((3,)),
        ],
        compiler_params=pltpu.CompilerParams(vmem_limit_bytes=4 << 20),
        name="pack",
    )(order, img_kv, stale_mant, stale_exp)
    blocks, late = gather_blocks(block[None])
    waited = blocks if late else []
    share = heads // 2
    part = share * (width // heads)
    gate, txt_q, txt_kv, turned, *state = pl.pallas_call(
        functools.partial(text_first_kernel, heads, share),
        out_shape=(
            pltpu.VMEM(gate_table.shape, f32),
            pltpu.VMEM(txt_q.shape, bf16),
            pltpu.VMEM(txt_kv.shape, bf16),
            pltpu.VMEM((rows, width), bf16),
            pltpu.VMEM((all_rows, part), f32),
            pltpu.VMEM((all_rows, part), f32),
        ),
        in_specs=[VMEM] + [HBM] * 4 + [VMEM] * len(waited),
        out_specs=[VMEM] * 6,
        scratch_shapes=[
            pltpu.VMEM(img_q.shape, img_q.dtype),
            pltpu.VMEM((share, all_rows, text_rows), bf16),
            pltpu.SemaphoreType.DMA((5,)),
        ],
        compiler_params=pltpu.CompilerParams(vmem_limit_bytes=16 << 20),
        name="text_first",
    )(order, img_q, txt_q, txt_kv, gate_table, *waited)
    if late:
        near = join(blocks, after=(turned,))
        blocks = [near, swap(near, 1)]
    rest = pl.pallas_call(
        functools.partial(text_second_kernel, heads, share),
        out_shape=(
            pltpu.VMEM((all_rows, width - part), f32),
            pltpu.VMEM((all_rows, width - part), f32),
        ),
        in_specs=[VMEM] * 3,
        out_specs=[VMEM] * 2,
        compiler_params=pltpu.CompilerParams(vmem_limit_bytes=16 << 20),
        name="text_second",
    )(txt_q, txt_kv, turned)
    states = (gate, txt_q, turned, *state, *rest)
    if late:
        far = join(late, after=())
        blocks += [far, swap(far, 1)]
    return pl.pallas_call(
        functools.partial(image_kernel, heads, share),
        out_shape=(
            jax.ShapeDtypeStruct(img_q.shape, bf16),
            jax.ShapeDtypeStruct(txt_q.shape, bf16),
        ),
        in_specs=[SMEM] + [VMEM] * (len(states) + len(blocks)),
        out_specs=(VMEM, VMEM),
        compiler_params=pltpu.CompilerParams(vmem_limit_bytes=32 << 20),
        name="image",
    )(timestep, *states, *blocks)


def solution(mesh):
    in_specs = (
        P(("groups", "patch"), None),
        P(None, ("groups", "patch"), None),
        P(None, ("groups", "patch"), None),
        P(None, ("groups", "patch"), None),
        P("groups", None),
        P(None, "groups", None),
        P(("groups", "patch")),
        P("groups"),
        P(),
    )
    out_specs = (P(("groups", "patch"), None), P("groups", None))
    return jax.shard_map(
        on_device, mesh=mesh, in_specs=in_specs, out_specs=out_specs, check_vma=False
    )
```

```python
import functools
import math

import jax
import jax.numpy as jnp
from jax import lax
from jax.experimental import pallas as pl
from jax.experimental.pallas import tpu as pltpu
from jax.sharding import PartitionSpec as P

VMEM = pl.BlockSpec(memory_space=pltpu.VMEM)
HBM = pl.BlockSpec(memory_space=pltpu.HBM)
SMEM = pl.BlockSpec(memory_space=pltpu.SMEM)
NT = (((1,), (1,)), ((), ()))
LOG2E = 1.4426950408889634
HIDDEN = -1e30
HOPS = ((2, 12), (8, 4), (4, 2))


def turn_tables(first, rows, head_dim):
    half = head_dim // 2
    lane = lax.broadcasted_iota(jnp.int32, (rows, head_dim), 1)
    row = lax.broadcasted_iota(jnp.int32, (rows, head_dim), 0)
    low = lane < half
    index = jnp.where(low, lane, lane - half).astype(jnp.float32)
    frequency = jnp.exp(index * (-math.log(10000.0) / half))
    angles = (first + row).astype(jnp.float32) * frequency
    sine = jnp.sin(angles)
    return jnp.cos(angles), jnp.where(low, -sine, sine)


def turn(x, cosine, sine):
    return x * cosine + pltpu.roll(x, x.shape[1] // 2, axis=1) * sine


def pack_kernel(order_ref, kv_hbm, mant_hbm, exp_hbm, block_ref, kv, mant, exp, sems):
    copies = [
        pltpu.make_async_copy(source, target, sems.at[i])
        for i, (source, target) in enumerate(((exp_hbm, exp), (kv_hbm, kv), (mant_hbm, mant)))
    ]
    for copy in copies:
        copy.start()
    rows, width = kv.shape[1:]
    heads = exp.shape[2]
    head_dim = width // heads
    cosine, sine = turn_tables(order_ref[...] * rows, rows, head_dim)
    for copy in copies:
        copy.wait()
    for which in range(2):
        power = jnp.exp2(exp[which].astype(jnp.float32))
        power = power.astype(jnp.bfloat16).astype(jnp.float32)
        for head in range(heads):
            span = slice(head * head_dim, (head + 1) * head_dim)
            fresh = kv[which, :, span].astype(jnp.float32)
            if which == 0:
                fresh = turn(fresh, cosine, sine)
            stale = mant[which, :, span].astype(jnp.float32) * power[:, head : head + 1]
            both = jnp.concatenate([fresh, stale], axis=0).astype(jnp.bfloat16)
            start = which * width + head * head_dim
            block_ref[:, start : start + head_dim] = both


def join_kernel(count, *refs):
    for i, block in enumerate(refs[:count]):
        refs[-1][i] = block[0]


def join(blocks, after=()):
    return pl.pallas_call(
        functools.partial(join_kernel, len(blocks)),
        out_shape=pltpu.VMEM((len(blocks),) + blocks[0].shape[1:], blocks[0].dtype),
        in_specs=[VMEM] * (len(blocks) + len(after)),
        out_specs=VMEM,
        compiler_params=pltpu.CompilerParams(vmem_limit_bytes=2 << 20),
        name="join",
    )(*blocks, *after)


def with_ones(values):
    return jnp.concatenate([values, jnp.ones_like(values)], axis=1)


def text_first_kernel(heads, share, order_ref, q_hbm, txt_q_hbm, txt_kv_hbm, gate_hbm, *refs):
    gate_ref, txt_q, txt_kv, turned_ref, mean_ref, level_ref, q, powers_ref, sems = refs[-9:]
    q_copy = pltpu.make_async_copy(q_hbm, q, sems.at[0])
    txt_q_copy = pltpu.make_async_copy(txt_q_hbm, txt_q, sems.at[1])
    keys_copy = pltpu.make_async_copy(txt_kv_hbm.at[0], txt_kv.at[0], sems.at[2])
    values_copy = pltpu.make_async_copy(txt_kv_hbm.at[1], txt_kv.at[1], sems.at[3])
    gate_copy = pltpu.make_async_copy(gate_hbm, gate_ref, sems.at[4])
    for copy in (q_copy, txt_q_copy, keys_copy, values_copy, gate_copy):
        copy.start()
    rows, width = q.shape
    head_dim = width // heads
    scale = head_dim ** (-0.5) * LOG2E
    cosine, sine = turn_tables(order_ref[...] * rows, rows, head_dim)
    q_copy.wait()
    for head in range(heads):
        span = slice(head * head_dim, (head + 1) * head_dim)
        turned = turn(q[:, span].astype(jnp.float32), cosine, sine)
        turned_ref[:, span] = turned.astype(jnp.bfloat16)
    txt_q_copy.wait()
    keys_copy.wait()
    for head in range(share):
        span = slice(head * head_dim, (head + 1) * head_dim)
        queries = jnp.concatenate([txt_q[:, span], turned_ref[:, span]], axis=0)
        scores = lax.dot_general(queries, txt_kv[0, :, span], NT, preferred_element_type=jnp.float32)
        scores = scores * scale
        highest = jnp.max(scores, axis=-1, keepdims=True)
        powers_ref[head] = jnp.exp2(scores - highest).astype(jnp.bfloat16)
        level_ref[:, span] = jnp.broadcast_to(highest, (highest.shape[0], head_dim))
    values_copy.wait()
    for head in range(share):
        span = slice(head * head_dim, (head + 1) * head_dim)
        summed = jnp.dot(
            powers_ref[head], with_ones(txt_kv[1, :, span]), preferred_element_type=jnp.float32
        )
        mean_ref[:, span] = summed[:, :head_dim] / summed[:, head_dim:]
        level_ref[:, span] = level_ref[:, span] + jnp.log2(summed[:, head_dim:])
    gate_copy.wait()


def text_second_kernel(heads, first, txt_q, txt_kv, turned_ref, mean_ref, level_ref):
    head_dim = txt_q.shape[1] // heads
    scale = head_dim ** (-0.5) * LOG2E
    for head in range(first, heads):
        span = slice(head * head_dim, (head + 1) * head_dim)
        here = slice((head - first) * head_dim, (head - first + 1) * head_dim)
        queries = jnp.concatenate([txt_q[:, span], turned_ref[:, span]], axis=0)
        scores = lax.dot_general(queries, txt_kv[0, :, span], NT, preferred_element_type=jnp.float32)
        scores = scores * scale
        highest = jnp.max(scores, axis=-1, keepdims=True)
        powers = jnp.exp2(scores - highest).astype(jnp.bfloat16)
        summed = jnp.dot(powers, with_ones(txt_kv[1, :, span]), preferred_element_type=jnp.float32)
        mean_ref[:, here] = summed[:, :head_dim] / summed[:, head_dim:]
        level_ref[:, here] = highest + jnp.log2(summed[:, head_dim:])


def image_kernel(heads, first, time_ref, gate_ref, txt_q_ref, turned_ref, *refs):
    states, blocks, (img_out_ref, txt_out_ref) = refs[:4], refs[4:-2], refs[-2:]
    time = time_ref[0]
    rows, width = img_out_ref.shape
    head_dim = width // heads
    text_rows = txt_q_ref.shape[0]
    scale = head_dim ** (-0.5) * LOG2E
    columns = 2 * rows * sum(block.shape[0] for block in blocks)
    column = lax.broadcasted_iota(jnp.int32, (rows, columns), 1)
    fresh = lax.rem(column, 2 * rows) < rows
    no_stale = jnp.where(fresh, 0.0, HIDDEN)
    no_fresh = jnp.where(fresh, HIDDEN, 0.0)
    image_mask = jnp.where(column < 2 * rows, no_stale, no_fresh)
    text_mask = no_stale[:1]
    for head in range(heads):
        span = slice(head * head_dim, (head + 1) * head_dim)
        mean_ref, level_ref = states[:2] if head < first else states[2:]
        place = head if head < first else head - first
        here = slice(place * head_dim, (place + 1) * head_dim)
        keys, values = (
            jnp.concatenate(
                [
                    block[i, :, start : start + head_dim]
                    for block in blocks
                    for i in range(block.shape[0])
                ],
                axis=0,
            )
            for start in (head * head_dim, width + head * head_dim)
        )
        queries = jnp.concatenate([txt_q_ref[:, span], turned_ref[:, span]], axis=0)
        scores = lax.dot_general(queries, keys, NT, preferred_element_type=jnp.float32)
        scores = jnp.concatenate(
            [scores[:text_rows] * scale + text_mask, scores[text_rows:] * scale + image_mask], axis=0
        )
        level = level_ref[:, here]
        highest = jnp.maximum(level, jnp.max(scores, axis=-1, keepdims=True))
        weight = jnp.exp2(level - highest)
        powers = jnp.exp2(scores - jnp.concatenate([highest] * (columns // head_dim), axis=1))
        summed = jnp.dot(
            powers.astype(jnp.bfloat16), with_ones(values), preferred_element_type=jnp.float32
        )
        result = (mean_ref[:, here] * weight + summed[:, :head_dim]) / (weight + summed[:, head_dim:])
        gate = gate_ref[time, :, span]
        txt_out_ref[:, span] = (result[:text_rows] * gate[1:2]).astype(jnp.bfloat16)
        img_out_ref[:, span] = (result[text_rows:] * gate[0:1]).astype(jnp.bfloat16)


def swap(x, even, odd=None):
    odd = even if odd is None else odd
    count = lax.axis_size("patch")
    pairs = [(i, i ^ (odd if i % 2 else even)) for i in range(count)]
    return lax.ppermute(x, "patch", pairs)


def gather_blocks(block):
    count = lax.axis_size("patch")
    if count == 16:
        one, two, three = (swap(block, *hop) for hop in HOPS)
        one_two = swap(one, *HOPS[1])
        one_three = swap(one, *HOPS[2])
        two_three = swap(two, *HOPS[2])
        all_three = swap(one_two, *HOPS[2])
        return [block, one, two, three], [one_two, one_three, two_three, all_three]
    if count & (count - 1) == 0:
        bit = count // 2
        while bit:
            block = jnp.concatenate([block, swap(block, bit)], axis=0)
            bit //= 2
        return [block], []
    blocks = [block]
    ring = [(i, (i + 1) % count) for i in range(count)]
    for _ in range(count - 1):
        blocks.append(lax.ppermute(blocks[-1], "patch", ring))
    return blocks, []


def on_device(img_q, img_kv, stale_mant, stale_exp, txt_q, txt_kv, order, timestep, gate_table):
    rows, width = img_q.shape
    heads = stale_exp.shape[2]
    text_rows = txt_q.shape[0]
    all_rows = text_rows + rows
    bf16, f32 = jnp.bfloat16, jnp.float32
    img_q, img_kv, stale_mant, stale_exp, gate_table, txt_q, txt_kv = (
        pltpu.with_memory_space_constraint(x, pltpu.HBM)
        for x in (img_q, img_kv, stale_mant, stale_exp, gate_table, txt_q, txt_kv)
    )
    order = order.reshape(1, 1)
    block = pl.pallas_call(
        pack_kernel,
        out_shape=pltpu.VMEM((2 * rows, 2 * width), bf16),
        in_specs=[VMEM] + [HBM] * 3,
        out_specs=VMEM,
        scratch_shapes=[
            pltpu.VMEM(img_kv.shape, img_kv.dtype),
            pltpu.VMEM(stale_mant.shape, stale_mant.dtype),
            pltpu.VMEM(stale_exp.shape, stale_exp.dtype),
            pltpu.SemaphoreType.DMA((3,)),
        ],
        compiler_params=pltpu.CompilerParams(vmem_limit_bytes=4 << 20),
        name="pack",
    )(order, img_kv, stale_mant, stale_exp)
    blocks, late = gather_blocks(block[None])
    waited = []
    if late:
        near = join(blocks)
        waited = [near]
    share = heads // 2
    part = share * (width // heads)
    gate, txt_q, txt_kv, turned, *state = pl.pallas_call(
        functools.partial(text_first_kernel, heads, share),
        out_shape=(
            pltpu.VMEM(gate_table.shape, f32),
            pltpu.VMEM(txt_q.shape, bf16),
            pltpu.VMEM(txt_kv.shape, bf16),
            pltpu.VMEM((rows, width), bf16),
            pltpu.VMEM((all_rows, part), f32),
            pltpu.VMEM((all_rows, part), f32),
        ),
        in_specs=[VMEM] + [HBM] * 4 + [VMEM] * len(waited),
        out_specs=[VMEM] * 6,
        scratch_shapes=[
            pltpu.VMEM(img_q.shape, img_q.dtype),
            pltpu.VMEM((share, all_rows, text_rows), bf16),
            pltpu.SemaphoreType.DMA((5,)),
        ],
        compiler_params=pltpu.CompilerParams(vmem_limit_bytes=16 << 20),
        name="text_first",
    )(order, img_q, txt_q, txt_kv, gate_table, *waited)
    if late:
        blocks = [near, swap(near, 1)]
    rest = pl.pallas_call(
        functools.partial(text_second_kernel, heads, share),
        out_shape=(
            pltpu.VMEM((all_rows, width - part), f32),
            pltpu.VMEM((all_rows, width - part), f32),
        ),
        in_specs=[VMEM] * 3,
        out_specs=[VMEM] * 2,
        compiler_params=pltpu.CompilerParams(vmem_limit_bytes=16 << 20),
        name="text_second",
    )(txt_q, txt_kv, turned)
    states = (gate, txt_q, turned, *state, *rest)
    if late:
        far = join(late, after=(turned,))
        blocks += [far, swap(far, 1)]
    return pl.pallas_call(
        functools.partial(image_kernel, heads, share),
        out_shape=(
            jax.ShapeDtypeStruct(img_q.shape, bf16),
            jax.ShapeDtypeStruct(txt_q.shape, bf16),
        ),
        in_specs=[SMEM] + [VMEM] * (len(states) + len(blocks)),
        out_specs=(VMEM, VMEM),
        compiler_params=pltpu.CompilerParams(vmem_limit_bytes=32 << 20),
        name="image",
    )(timestep, *states, *blocks)


def solution(mesh):
    in_specs = (
        P(("groups", "patch"), None),
        P(None, ("groups", "patch"), None),
        P(None, ("groups", "patch"), None),
        P(None, ("groups", "patch"), None),
        P("groups", None),
        P(None, "groups", None),
        P(("groups", "patch")),
        P("groups"),
        P(),
    )
    out_specs = (P(("groups", "patch"), None), P("groups", None))
    return jax.shard_map(
        on_device, mesh=mesh, in_specs=in_specs, out_specs=out_specs, check_vma=False
    )
```
